128 devices in a mesh: grp: 2 (over core), ep: 64 (over z, y, x).
Axes of the slice: x: 4, y: 4, z: 4, core: 2. Of those that a mesh axis runs over, the one named last changes fastest.
Arguments:
- hidden_states: bfloat16 [2, 512, 7168], P(None, ('grp', 'ep')), may hold values from -6 to 6
- expert_routes: int32 [2, 512, 8], P(None, ('grp', 'ep')), may hold values from 0 to 15, all different within a row; in each aligned block of 4 rows (0 to 3, 4 to 7, ..., all dimensions but the last counted through in order) at most 4 rows name the same one
- route_gates: bfloat16 [2, 512, 8], P(None, ('grp', 'ep')), may hold values from 0.099609375 to 0.59765625
- gate_weights: bfloat16 [64, 7168, 512], P('ep', None, 'grp'), may hold values from -0.0625 to 0.0625
- up_weights: bfloat16 [64, 7168, 512], P('ep', None, 'grp'), may hold values from -0.0625 to 0.0625
- down_weights: bfloat16 [64, 512, 7168], P('ep', 'grp'), may hold values from -0.125 to 0.125
Outputs:
- mixed: bfloat16 [2, 512, 7168], P(None, ('grp', 'ep'))
The draws below stay inside these ranges and needn't reach their ends.
Inputs may be any that keep to these rules, and one draw needn't show every extreme that they name: `expert_routes`: each token names 8 different experts. Among the tokens of one block of 4 tokens of a step, no expert is named more than 4 times, and in every draw some expert is named exactly 4 times in some block.
All inputs are finite; a program needn't handle non-finite values.
Results may differ from the reference program's by a relative error of at most 0.015.
Values may be sent and summed in bfloat16 or wider, within the bound.
A program may use at most 128 MiB of HBM per device.

```python
import math
import jax
import jax.numpy as jnp
import numpy as np
from jax import lax

D = 7168
HID = 2048
HID_DEV = 256
STEPS = 2
TOK_DEV = 4
SPLIT = 4
EXPERTS = 16
TOPK = 8
CAP = 4
TOKENS = 512
N_GRP = 2
N_EP = 64


def shard_levels(key, extent, pieces, low, top_value):
    def one(position, shards_of):
        heights = jax.random.uniform(jax.random.fold_in(jax.random.fold_in(key, 6), position), (shards_of,), jnp.float32, low / len(pieces), top_value / len(pieces))
        return jnp.repeat(jnp.exp(heights), extent[position] // shards_of).reshape((-1,) + (1,) * (len(extent) - position - 1))

    factor_of = one(*pieces[0])
    for cut in pieces[1:]:
        factor_of = factor_of * one(*cut)
    return factor_of


def routed_block(own_key, own, number, rows, number_of, top, reach, slope):
    ranking = jax.random.permutation(own_key, number_of)
    crowded, ordinary = load_shares(number_of, rows * top, reach, slope, True), load_shares(number_of, rows * top, reach, slope, False)
    places = jnp.arange(number_of)

    def named(sizes, offset_by):
        used = int((sizes > 0).sum())
        fixed = max(1, used // 4)
        shifted = fixed + (places - fixed + offset_by * (used - fixed)) % max(1, number_of - fixed)
        return jnp.zeros((number_of,), jnp.int32).at[ranking[jnp.where(places < fixed, places, shifted)]].set(jnp.asarray(sizes, jnp.int32))

    sizes = jnp.where(number % 4 == 0, named(crowded, number // 4), named(ordinary, number - number // 4 - 1))
    mixed = jax.random.permutation(jax.random.fold_in(own, 3), number_of)
    source_of, sink = mixed[0:number_of // 2 * 2:2], mixed[1:number_of // 2 * 2:2]
    room = jnp.minimum(sizes[source_of] - 1, reach - sizes[sink]) // 2
    room = jnp.where((source_of == ranking[0]) | (sink == ranking[0]) | (sizes[sink] == 0), 0, jnp.maximum(room, 0))
    shifted = jax.random.randint(jax.random.fold_in(own, 4), (number_of // 2,), 0, 1 << 20) % (room + 1)
    sizes = sizes.at[source_of].add(-shifted).at[sink].add(shifted)
    labels = jnp.searchsorted(jnp.cumsum(sizes), jnp.arange(rows * top), side="right").astype(jnp.int32)
    listing = labels.reshape(top, rows).T
    listing = listing[jax.random.permutation(jax.random.fold_in(own, 1), rows)]
    offset_by = jax.random.randint(jax.random.fold_in(own, 2), (rows, 1), 0, top)
    return jnp.take_along_axis(listing, (jnp.arange(top)[None, :] + offset_by) % top, axis=1)


def load_shares(amount, total, reach, slope, full):
    portions = [(1 << 20) // math.isqrt(rank ** slope) + 1 for rank in range(1, amount + 1)]
    largest = reach if full else min(reach, max(-(-total // amount), total * portions[0] // sum(portions)))
    least = 1 if total - largest >= amount - 1 else 0
    counts, spare = [largest] + [least] * (amount - 1), total - largest - least * (amount - 1)
    while spare > 0:
        candidates = [i for i in range(1, amount) if counts[i] < largest] or [i for i in range(1, amount) if counts[i] < reach]
        pool, remaining = sum([portions[i] for i in candidates]), spare
        for i in candidates:
            more = min(reach - counts[i], max(1, remaining * portions[i] // pool), spare)
            counts[i] = counts[i] + more
            spare = spare - more
    return np.array(counts)


def scatter_about(rng, dims, width, most, split=(), held_as=jnp.bfloat16):
    gain = shard_levels(rng, dims, split, -0.22, 0.18) if split else 1.0
    entries = jax.random.normal(rng, dims, jnp.float32) * width * gain
    return jnp.minimum(jnp.maximum(entries, -most), most).astype(held_as)


def setup_inputs(seed: int = 0) -> dict:
    arg_keys = jax.random.split(jax.random.key(seed), 7)
    hidden_states = scatter_about(arg_keys[0], (STEPS, TOKENS, D), 1.0, 6.0, ((1, 128),))
    expert_routes_keys = jax.random.split(jax.random.fold_in(arg_keys[1], 1), STEPS * TOKENS // TOK_DEV)
    expert_routes_turns = jax.random.permutation(jax.random.fold_in(arg_keys[1], 3), STEPS * TOKENS // TOK_DEV)
    expert_routes = jax.vmap(lambda own, number: routed_block(jax.random.fold_in(arg_keys[1], 2), own, number, TOK_DEV, EXPERTS, TOPK, CAP, 2))(expert_routes_keys, expert_routes_turns).reshape((STEPS, TOKENS, TOPK))
    route_gates = jnp.clip(0.099609375 + 0.49804688 * jax.random.uniform(arg_keys[2], (STEPS, TOKENS, TOPK), jnp.float32) ** shard_levels(arg_keys[2], (STEPS, TOKENS, TOPK), ((1, 128),), -0.2, 0.2), 0.099609375, 0.59765625).astype(jnp.bfloat16)
    gate_weights = scatter_about(arg_keys[3], (EXPERTS * SPLIT, D, N_GRP * HID_DEV), D ** -0.5, 0.0625, ((0, 64), (2, 2)))
    up_weights = scatter_about(arg_keys[4], (EXPERTS * SPLIT, D, N_GRP * HID_DEV), D ** -0.5, 0.0625, ((0, 64), (2, 2)))
    down_weights = scatter_about(arg_keys[5], (EXPERTS * SPLIT, N_GRP * HID_DEV, D), HID ** -0.5, 0.125, ((0, 64), (1, 2)))
    return {"hidden_states": hidden_states, "expert_routes": expert_routes, "route_gates": route_gates, "gate_weights": gate_weights, "up_weights": up_weights, "down_weights": down_weights}


def tables(routes, gates, experts, capacity):
    tok_count, topk = routes.shape
    flat_routes = routes.reshape(-1)
    one_hot = (flat_routes[:, None] == jnp.arange(experts, dtype=jnp.int32)[None, :]).astype(jnp.int32)
    before = jnp.cumsum(one_hot, axis=0) - one_hot
    slot_place = jnp.sum(before * one_hot, axis=1).astype(jnp.int32)
    column = flat_routes * capacity + slot_place
    picked = column[:, None] == jnp.arange(experts * capacity, dtype=jnp.int32)[None, :]
    picked = picked.reshape(tok_count, topk, experts * capacity)
    dispatch_table = jnp.any(picked, axis=1)
    combine_table = jnp.sum(picked.astype(jnp.float32) * gates.astype(jnp.float32)[:, :, None], axis=1)
    return dispatch_table, combine_table


def reference(hidden_states, expert_routes, route_gates, gate_weights, up_weights, down_weights):
    blocks = N_GRP * N_EP
    span = N_GRP * HID_DEV
    gate_split = gate_weights.reshape(EXPERTS, SPLIT, D, span)
    up_split = up_weights.reshape(EXPERTS, SPLIT, D, span)
    down_split = down_weights.reshape(EXPERTS, SPLIT, span, D)
    step_outputs = []
    for step_index in range(STEPS):
        token_rows = hidden_states[step_index].reshape(blocks, TOK_DEV, D)
        route_rows = expert_routes[step_index].reshape(blocks, TOK_DEV, TOPK)
        gate_rows = route_gates[step_index].reshape(blocks, TOK_DEV, TOPK)
        dispatch_table, combine_table = jax.vmap(lambda r, g: tables(r, g, EXPERTS, CAP))(route_rows, gate_rows)
        outgoing = jnp.einsum('btm,btd->bmd', dispatch_table.astype(jnp.bfloat16), token_rows, preferred_element_type=jnp.float32).astype(jnp.bfloat16)
        outgoing = outgoing.reshape(blocks, EXPERTS, CAP, D).transpose(1, 0, 2, 3).reshape(EXPERTS, blocks * CAP, D)

        def one_expert(operands):
            rows, gate_w, up_w, down_w = operands
            total = jnp.zeros((rows.shape[0], D), jnp.float32)
            for split_index in range(SPLIT):
                gate_proj = jnp.dot(rows, gate_w[split_index], preferred_element_type=jnp.float32)
                up_proj = jnp.dot(rows, up_w[split_index], preferred_element_type=jnp.float32)
                act = (jax.nn.silu(gate_proj) * up_proj).astype(jnp.bfloat16)
                inner = jnp.zeros((rows.shape[0], D), jnp.float32)
                for part_index in range(N_GRP):
                    lower = part_index * HID_DEV
                    part = jnp.dot(act[:, lower:lower + HID_DEV], down_w[split_index, lower:lower + HID_DEV], preferred_element_type=jnp.float32).astype(jnp.bfloat16)
                    part = lax.optimization_barrier(part)
                    inner = inner + part.astype(jnp.float32)
                partial_value = lax.optimization_barrier(inner.astype(jnp.bfloat16))
                total = total + partial_value.astype(jnp.float32)
            return total.astype(jnp.bfloat16)

        expert_out = lax.map(one_expert, (outgoing, gate_split, up_split, down_split))
        expert_out = expert_out.reshape(EXPERTS, blocks, CAP, D).transpose(1, 0, 2, 3).reshape(blocks, EXPERTS * CAP, D)
        mixed = jnp.einsum('btm,bmd->btd', combine_table, expert_out.astype(jnp.float32), precision=lax.Precision.HIGHEST)
        step_outputs.append(mixed.astype(jnp.bfloat16).reshape(blocks * TOK_DEV, D))
    return jnp.stack(step_outputs, axis=0)
```

```python
import jax
import jax.numpy as jnp
from jax import lax
from jax.sharding import PartitionSpec as P

EXPERTS = 16
PAD = 128


def expert_weights(routes, gates):
    picked = routes[..., None] == jnp.arange(EXPERTS, dtype=jnp.int32)
    return jnp.sum(
        jnp.where(picked, gates.astype(jnp.float32)[..., None], 0.0), axis=-2
    ).astype(jnp.bfloat16)


def body(hidden_states, expert_routes, route_gates, gate_weights, up_weights, down_weights):
    steps, tok, width = hidden_states.shape
    holders = lax.axis_size("ep") // EXPERTS
    mine = lax.axis_index("ep") // holders
    table = expert_weights(expert_routes, route_gates)
    table = jnp.pad(table, ((0, 0), (0, 0), (0, PAD - EXPERTS)))
    rows = jnp.concatenate([hidden_states, table], axis=-1)
    outs = []
    for s in range(steps):
        full = lax.all_gather(rows[s], ("grp", "ep"), axis=0, tiled=True)
        x = full[:, :width]
        weight = jnp.sum(
            jnp.where(
                jnp.arange(PAD) == mine, full[:, width:].astype(jnp.float32), 0.0
            ),
            axis=1,
            keepdims=True,
        )
        gate = jnp.dot(x, gate_weights[0], preferred_element_type=jnp.float32)
        up = jnp.dot(x, up_weights[0], preferred_element_type=jnp.float32)
        act = (jax.nn.silu(gate) * up).astype(jnp.bfloat16)
        part = jnp.dot(act, down_weights[0], preferred_element_type=jnp.float32)
        part = (part * weight).astype(jnp.bfloat16)
        outs.append(lax.psum_scatter(part, ("grp", "ep"), scatter_dimension=0, tiled=True))
    return jnp.stack(outs, axis=0)


def solution(mesh):
    return jax.shard_map(
        body,
        mesh=mesh,
        in_specs=(
            P(None, ("grp", "ep"), None),
            P(None, ("grp", "ep"), None),
            P(None, ("grp", "ep"), None),
            P("ep", None, "grp"),
            P("ep", None, "grp"),
            P("ep", "grp", None),
        ),
        out_specs=P(None, ("grp", "ep"), None),
        check_vma=False,
    )
```

```python
import jax
import jax.numpy as jnp
from jax import lax
from jax.experimental import pallas as pl
from jax.experimental.pallas import tpu as pltpu
from jax.sharding import PartitionSpec as P

EXPERTS = 16
LANE = 128
TILE = 16
UNITS = 28
HALF = UNITS * LANE
HALF_T = HALF + LANE
HIDDEN = 256
MESH = pl.DeviceIdType.MESH
F32 = jnp.float32
BF16 = jnp.bfloat16

PARTS = ((0, 10, (2, 1, 0)), (10, 9, (0, 2, 1)), (19, 9, (1, 0, 2)))
TABLE_PART = 2


def part_units(p, table):
    first, count, _ = PARTS[p]
    return first, count + (1 if table and p == TABLE_PART else 0)


def halves(p, table):
    first, count = part_units(p, table)
    left = (count + 1) // 2
    return (first, left), (first + left, count - left)


def kernel(
    hs, routes, gates, wg_hbm, wu_hbm, wd_hbm,
    out,
    X, wgu, wd, h, act, zero_send, zero_recv, last_send, last_recv, R0,
    R30, R31, R32, R20, R21, R22, R10, R11, R12,
    w_sem, g_send, g_recv, b_send, b_recv, s_send, s_recv, c_send, c_recv, e_send, e_recv,
):
    R = {3: (R30, R31, R32), 2: (R20, R21, R22), 1: (R10, R11, R12)}
    core = lax.axis_index("grp")
    ep = lax.axis_index("ep")
    me = (ep // 16, (ep // 4) % 4, ep % 4)
    sibling = (1 - core, ep)
    scale = (16, 4, 1)

    def peer(axis, delta):
        moved = lax.rem(me[axis] + delta, 4)
        return (core, ep + (moved - me[axis]) * scale[axis])

    def place(axis, delta):
        return lax.rem(me[axis] + delta, 4)

    weights = [
        pltpu.make_async_copy(wg_hbm.at[0], wgu.at[:, pl.ds(0, HIDDEN)], w_sem.at[0]),
        pltpu.make_async_copy(wu_hbm.at[0], wgu.at[:, pl.ds(HIDDEN, HIDDEN)], w_sem.at[1]),
        pltpu.make_async_copy(wd_hbm.at[0], wd, w_sem.at[2]),
    ]
    for copy in weights:
        copy.start()

    barrier = pltpu.get_barrier_semaphore()
    for axis in range(3):
        for delta in (1, 3):
            pl.semaphore_signal(barrier, inc=1, device_id=peer(axis, delta), device_id_type=MESH)
    pl.semaphore_signal(barrier, inc=1, device_id=sibling, device_id_type=MESH)

    lane = lax.broadcasted_iota(jnp.int32, (4, LANE), 1)

    def own_rows(c):
        at = pl.multiple_of(c * HALF, LANE)
        return jnp.concatenate(
            [hs[s, :, pl.ds(at, HALF)].astype(F32) for s in range(2)], axis=0
        )

    tables = []
    for s in range(2):
        total = jnp.zeros((4, LANE), F32)
        for k in range(8):
            total += jnp.where(
                lane == routes[s, :, k : k + 1], gates[s, :, k : k + 1].astype(F32), 0.0
            )
        tables.append(total)
    table = jnp.concatenate(tables, axis=0)

    zero_send[:, pl.ds(0, HALF)] = own_rows(1 - core)
    zero_send[:, pl.ds(HALF, LANE)] = table
    pl.semaphore_wait(barrier, 7)
    swap = pltpu.make_async_remote_copy(
        src_ref=zero_send, dst_ref=zero_recv, send_sem=e_send.at[0], recv_sem=e_recv.at[0],
        device_id=sibling, device_id_type=MESH,
    )
    swap.start()
    h[...] = jnp.zeros_like(h)
    base = pl.multiple_of(core * HALF_T, LANE)
    mine = jnp.concatenate([own_rows(core), table], axis=1)
    swap.wait()
    theirs = zero_recv[...]
    first = core == 0
    X[me[0], me[1], me[2], :, pl.ds(base, HALF_T)] = jnp.concatenate(
        [jnp.where(first, mine, theirs), jnp.where(first, theirs, mine)], axis=0
    ).astype(BF16)

    def block(p, stage, j, c, first_unit, count):
        order = PARTS[p][2]
        index = []
        for axis in range(3):
            if axis == order[stage - 1]:
                index.append(pl.ds(j, 1))
            elif axis in order[: stage - 1]:
                index.append(pl.ds(0, 4))
            else:
                index.append(pl.ds(me[axis], 1))
        at = pl.multiple_of(c * HALF_T + first_unit * LANE, LANE)
        return tuple(index) + (pl.ds(0, TILE), pl.ds(at, count * LANE))

    def gather_copy(p, stage, k, j, half, device):
        ref = X.at[block(p, stage, j, core, *half)]
        at = ((stage - 1) * 3 + p) * 6 + k
        return pltpu.make_async_remote_copy(
            src_ref=ref, dst_ref=ref, send_sem=g_send.at[at], recv_sem=g_recv.at[at],
            device_id=device, device_id_type=MESH,
        )

    def gather_message(p, stage, k, arriving):
        axis = PARTS[p][2][stage - 1]
        a, b = halves(p, True)
        offset, half, to = (
            (0, a, 1), (0, b, 1), (0, b, 3), (0, a, 3), (3, a, 1), (1, b, 3)
        )[k]
        if arriving:
            offset = offset + (3 if to == 1 else 1)
        return gather_copy(p, stage, k, place(axis, offset), half, peer(axis, to))

    def gather_start(p, stage):
        for k in (0, 2, 1, 3):
            gather_message(p, stage, k, False).start()

    def gather_arrived(p, stage, k):
        gather_message(p, stage, k, True).wait_recv()

    def gather_forward(p, stage):
        gather_arrived(p, stage, 0)
        gather_message(p, stage, 4, False).start()
        gather_arrived(p, stage, 2)
        gather_message(p, stage, 5, False).start()

    for stage in (1, 2):
        for p in range(3):
            gather_start(p, stage)
        for p in range(3):
            gather_forward(p, stage)
        for p in range(3):
            for k in (1, 3, 4, 5):
                gather_arrived(p, stage, k)

    def pass_copy(p, k, c):
        axis = PARTS[p][2][2]
        offset = (0, 3, 1, 2, 2)[k]
        part = (PARTS[p][0], PARTS[p][1])
        cut = (part, part, part) + halves(p, False)
        ref = X.at[block(p, 3, place(axis, offset), c, *cut[k])]
        at = p * 5 + k
        return pltpu.make_async_remote_copy(
            src_ref=ref, dst_ref=ref, send_sem=s_send.at[at], recv_sem=s_recv.at[at],
            device_id=sibling, device_id_type=MESH,
        )

    def hidden_index(p, j):
        axis = PARTS[p][2][2]
        return tuple(pl.ds(j, 1) if a == axis else pl.ds(0, 4) for a in range(3))

    def multiply(p, offset, c):
        first_unit, count, order = PARTS[p]
        j = place(order[2], offset)
        rows = X[block(p, 3, j, c, first_unit, count)].reshape(16 * TILE, count * LANE)
        at = pl.multiple_of(c * HALF + first_unit * LANE, LANE)
        where = hidden_index(p, j)
        found = jnp.dot(rows, wgu[pl.ds(at, count * LANE), :], preferred_element_type=F32)
        h[where] += found.reshape(h[where].shape)

    for p in range(3):
        gather_start(p, 3)
    for p in range(3):
        pass_copy(p, 0, core).start()
    weights[0].wait()
    weights[1].wait()
    for p in range(3):
        multiply(p, 0, core)
    for p in range(3):
        pass_copy(p, 0, 1 - core).wait_recv()
        multiply(p, 0, 1 - core)
    for p in range(3):
        gather_forward(p, 3)
    for p in range(3):
        gather_arrived(p, 3, 1)
        pass_copy(p, 1, core).start()
        gather_arrived(p, 3, 3)
        pass_copy(p, 2, core).start()
    for p in range(3):
        multiply(p, 3, core)
        multiply(p, 1, core)
    for p in range(3):
        pass_copy(p, 1, 1 - core).wait_recv()
        multiply(p, 3, 1 - core)
        pass_copy(p, 2, 1 - core).wait_recv()
        multiply(p, 1, 1 - core)
    for p in range(3):
        gather_arrived(p, 3, 4)
        pass_copy(p, 3, core).start()
        gather_arrived(p, 3, 5)
        pass_copy(p, 4, core).start()
    for p in range(3):
        multiply(p, 2, core)
    for p in range(3):
        pass_copy(p, 3, 1 - core).wait_recv()
        pass_copy(p, 4, 1 - core).wait_recv()
        multiply(p, 2, 1 - core)

    chosen = (lax.broadcasted_iota(jnp.int32, (LANE, HIDDEN), 0) == ep // 4).astype(BF16)
    table_at = pl.multiple_of(base + HALF, LANE)

    def activate(i, carry):
        rows = X[i, :, :, :, pl.ds(table_at, LANE)].reshape(16 * TILE, LANE)
        scaled = jnp.dot(rows, chosen, preferred_element_type=F32)
        both = h[i].reshape(16 * TILE, 2 * HIDDEN)
        gate, up = both[:, :HIDDEN], both[:, HIDDEN:]
        value = gate / (1.0 + jnp.exp(-gate)) * up * scaled
        act[i] = value.astype(BF16).reshape(4, 4, TILE, HIDDEN)
        return carry

    lax.fori_loop(0, 4, activate, 0)

    for stage in (1, 2, 3):
        for p in range(3):
            for k in range(6):
                gather_message(p, stage, k, False).wait_send()
    for p in range(3):
        for k in range(5):
            pass_copy(p, k, core).wait_send()
    weights[2].wait()

    def down(p, offset, c):
        first_unit, count, order = PARTS[p]
        rows = act[hidden_index(p, place(order[2], offset))].reshape(16 * TILE, HIDDEN)
        at = pl.multiple_of(c * HALF + first_unit * LANE, LANE)
        return jnp.dot(rows, wd[:, pl.ds(at, count * LANE)], preferred_element_type=F32)

    def cross_copy(p, offset, c):
        first_unit, count, order = PARTS[p]
        j = place(order[2], offset)
        where = block(p, 3, j, c, first_unit, count)
        to = hidden_index(p, j) + (pl.ds(0, TILE), pl.ds(first_unit * LANE, count * LANE))
        return pltpu.make_async_remote_copy(
            src_ref=X.at[where], dst_ref=R0.at[to],
            send_sem=c_send.at[p * 4 + offset], recv_sem=c_recv.at[p * 4 + offset],
            device_id=sibling, device_id_type=MESH,
        )

    def theirs_out(p, offset):
        first_unit, count, order = PARTS[p]
        where = block(p, 3, place(order[2], offset), 1 - core, first_unit, count)
        X[where] = down(p, offset, 1 - core).astype(BF16).reshape(X[where].shape)
        cross_copy(p, offset, 1 - core).start()

    def mine_out(p, offset):
        first_unit, count, order = PARTS[p]
        j = place(order[2], offset)
        where = block(p, 3, j, core, first_unit, count)
        found = down(p, offset, core)
        cross_copy(p, offset, core).wait_recv()
        to = hidden_index(p, j) + (pl.ds(0, TILE), pl.ds(first_unit * LANE, count * LANE))
        X[where] = (found.reshape(X[where].shape) + R0[to].astype(F32)).astype(BF16)

    def scatter_message(p, stage, k, arriving=False):
        order = PARTS[p][2]
        axis = order[stage - 1]
        a, b = halves(p, False)
        offset, half, to, slot = (
            (2, a, 1, 0), (2, b, 3, 0), (1, b, 1, 1), (3, a, 3, 2), (1, a, 1, 1), (3, b, 3, 2)
        )[k]
        src = X.at[block(p, stage, place(axis, offset), core, *half)]
        buffer = R[stage][p]
        span = (pl.ds((half[0] - PARTS[p][0]) * LANE, half[1] * LANE),)
        dst = buffer.at[(slot, slice(None), slice(None), slice(None), slice(None)) + span]
        at = ((stage - 1) * 3 + p) * 6 + k
        return pltpu.make_async_remote_copy(
            src_ref=src, dst_ref=dst, send_sem=b_send.at[at], recv_sem=b_recv.at[at],
            device_id=peer(axis, to), device_id_type=MESH,
        )

    def accumulate(p, stage, offset, half, slots):
        order = PARTS[p][2]
        j = place(order[stage - 1], offset)
        where = block(p, stage, j, core, *half)
        span = pl.ds((half[0] - PARTS[p][0]) * LANE, half[1] * LANE)
        buffer = R[stage][p]
        loops = [a for a in range(3) if a in order[: stage - 1]]

        def add(i, carry):
            at, frm = list(where), [slice(None)] * 3
            if loops:
                at[loops[0]] = pl.ds(i, 1)
                frm[loops[0]] = pl.ds(i, 1)
            at = tuple(at)
            total = X[at].astype(F32)
            for slot in slots:
                total += buffer[(slot,) + tuple(frm) + (slice(None), span)].astype(F32)
            X[at] = total.astype(BF16)
            return carry

        if loops:
            lax.fori_loop(0, 4, add, 0)
        else:
            add(0, 0)

    def scatter_forward(p, stage):
        a, b = halves(p, False)
        scatter_message(p, stage, 0).wait_recv()
        accumulate(p, stage, 1, a, (0,))
        scatter_message(p, stage, 4).start()
        scatter_message(p, stage, 1).wait_recv()
        accumulate(p, stage, 3, b, (0,))
        scatter_message(p, stage, 5).start()

    def scatter_finish(p, stage):
        for k in (2, 3, 4, 5):
            scatter_message(p, stage, k).wait_recv()
        if stage > 1:
            for half in halves(p, False):
                accumulate(p, stage, 0, half, (1, 2))

    for p in range(3):
        theirs_out(p, 2)
    for p in range(3):
        mine_out(p, 2)
        scatter_message(p, 3, 0).start()
        scatter_message(p, 3, 1).start()
    for p in range(3):
        theirs_out(p, 1)
        theirs_out(p, 3)
    for p in range(3):
        mine_out(p, 1)
        scatter_message(p, 3, 2).start()
        mine_out(p, 3)
        scatter_message(p, 3, 3).start()
    for p in range(3):
        scatter_forward(p, 3)
    for p in range(3):
        theirs_out(p, 0)
    for p in range(3):
        mine_out(p, 0)
    for p in range(3):
        scatter_finish(p, 3)
    for stage in (2, 1):
        for p in range(3):
            for k in (0, 1, 2, 3):
                scatter_message(p, stage, k).start()
        for p in range(3):
            scatter_forward(p, stage)
        for p in range(3):
            scatter_finish(p, stage)

    pieces = []
    for p in range(3):
        first_unit, count, order = PARTS[p]
        where = block(p, 1, me[order[0]], core, first_unit, count)
        total = X[where].astype(F32).reshape(TILE, count * LANE)
        for slot in (1, 2):
            total += R[1][p][slot].astype(F32).reshape(TILE, count * LANE)
        pieces.append(total)
    tile = jnp.concatenate(pieces, axis=1)
    last_send[...] = jnp.where(first, tile[8:], tile[:8])
    swap_back = pltpu.make_async_remote_copy(
        src_ref=last_send, dst_ref=last_recv, send_sem=e_send.at[1], recv_sem=e_recv.at[1],
        device_id=sibling, device_id_type=MESH,
    )
    swap_back.start()
    kept = jnp.where(first, tile[:8], tile[8:]).astype(BF16)
    at = pl.multiple_of(core * HALF, LANE)
    for s in range(2):
        out[s, :, pl.ds(at, HALF)] = kept[4 * s : 4 * s + 4]
    for stage in (1, 2, 3):
        for p in range(3):
            for k in range(6):
                scatter_message(p, stage, k).wait_send()
    for p in range(3):
        for offset in range(4):
            cross_copy(p, offset, 1 - core).wait_send()
    swap_back.wait()
    other = last_recv[...].astype(BF16)
    at = pl.multiple_of((1 - core) * HALF, LANE)
    for s in range(2):
        out[s, :, pl.ds(at, HALF)] = other[4 * s : 4 * s + 4]


def scatter_shapes():
    shapes = []
    for stage in (3, 2, 1):
        for p in range(3):
            order = PARTS[p][2]
            dims = tuple(4 if a in order[: stage - 1] else 1 for a in range(3))
            shapes.append(pltpu.VMEM((3,) + dims + (TILE, PARTS[p][1] * LANE), BF16))
    return shapes


def body(hidden_states, expert_routes, route_gates, gate_weights, up_weights, down_weights):
    width = hidden_states.shape[2]
    dma = pltpu.SemaphoreType.DMA
    vmem = pl.BlockSpec(memory_space=pltpu.VMEM)
    hbm = pl.BlockSpec(memory_space=pl.ANY)
    return pl.pallas_call(
        kernel,
        out_shape=jax.ShapeDtypeStruct(hidden_states.shape, BF16),
        in_specs=[vmem, vmem, vmem, hbm, hbm, hbm],
        out_specs=vmem,
        scratch_shapes=[
            pltpu.VMEM((4, 4, 4, TILE, 2 * HALF_T), BF16),
            pltpu.VMEM((width, 2 * HIDDEN), BF16),
            pltpu.VMEM((HIDDEN, width), BF16),
            pltpu.VMEM((4, 4, 4, TILE, 2 * HIDDEN), F32),
            pltpu.VMEM((4, 4, 4, TILE, HIDDEN), BF16),
            pltpu.VMEM((8, HALF_T), F32),
            pltpu.VMEM((8, HALF_T), F32),
            pltpu.VMEM((8, HALF), F32),
            pltpu.VMEM((8, HALF), F32),
            pltpu.VMEM((4, 4, 4, TILE, HALF), BF16),
            *scatter_shapes(),
            dma((3,)),
            dma((54,)), dma((54,)),
            dma((54,)), dma((54,)),
            dma((15,)), dma((15,)),
            dma((12,)), dma((12,)),
            dma((2,)), dma((2,)),
        ],
        compiler_params=pltpu.CompilerParams(
            collective_id=0, has_side_effects=True, vmem_limit_bytes=60 * 1024 * 1024
        ),
        cost_estimate=pl.CostEstimate(
            flops=11_300_000_000, bytes_accessed=12_000_000, transcendentals=262144
        ),
    )(hidden_states, expert_routes, route_gates, gate_weights, up_weights, down_weights)


def solution(mesh):
    return jax.shard_map(
        body,
        mesh=mesh,
        in_specs=(
            P(None, ("grp", "ep"), None),
            P(None, ("grp", "ep"), None),
            P(None, ("grp", "ep"), None),
            P("ep", None, "grp"),
            P("ep", None, "grp"),
            P("ep", "grp", None),
        ),
        out_specs=P(None, ("grp", "ep"), None),
        check_vma=False,
    )
```

```python
import jax
import jax.numpy as jnp
from jax import lax
from jax.experimental import pallas as pl
from jax.experimental.pallas import tpu as pltpu
from jax.sharding import PartitionSpec as P

LANE = 128
TILE = 8
UNITS = 28
HALF = UNITS * LANE
HALF_T = HALF + LANE
HIDDEN = 256
STEPS = 2
MESH = pl.DeviceIdType.MESH
F32 = jnp.float32
BF16 = jnp.bfloat16

PARTS = (
    ((0, 10, (2, 1, 0)), (10, 9, (0, 2, 1)), (19, 9, (1, 0, 2))),
    ((0, 10, (0, 2, 1)), (10, 9, (1, 0, 2)), (19, 9, (2, 1, 0))),
)
TABLE_PART = 2
N_PARTS = 3
G_SENDS, G_RECVS, B_SENDS, B_RECVS = 4, 12, 4, 15
PAIRS = tuple((s, p) for s in range(STEPS) for p in range(N_PARTS))


def part_units(q, table):
    first, count, _ = PARTS[q[0]][q[1]]
    return first, count + (1 if table and q[1] == TABLE_PART else 0)


def halves(q, table):
    first, count = part_units(q, table)
    left = (count + 1) // 2
    return (first, left), (first + left, count - left)


def kernel(
    hs, routes, gates, wg_hbm, wu_hbm, wd_hbm,
    out,
    X, wgu, wd, h, act, zero_send, zero_recv, last_send, last_recv, R0,
    *rest,
):
    n = len(PAIRS)
    R3, R2, R1 = (dict(zip(PAIRS, rest[i * n : (i + 1) * n])) for i in range(3))
    w_sem, e_send, e_recv, g_send, g_recv, b_send, b_recv = rest[3 * n :]
    core = lax.axis_index("grp")
    ep = lax.axis_index("ep")
    me = (ep // 16, (ep // 4) % 4, ep % 4)
    sibling = (1 - core, ep)
    scale = (16, 4, 1)
    parts = range(N_PARTS)

    spots = [[lax.rem(me[axis] + d, 4) for d in range(4)] for axis in range(3)]
    peers = [
        [(core, ep + (spots[axis][d] - me[axis]) * scale[axis]) for d in range(4)] for axis in range(3)
    ]

    def place(axis, delta):
        return spots[axis][delta % 4]

    def peer(axis, delta):
        return peers[axis][delta]

    weights = [
        pltpu.make_async_copy(wg_hbm.at[0], wgu.at[:, pl.ds(0, HIDDEN)], w_sem.at[0]),
        pltpu.make_async_copy(wu_hbm.at[0], wgu.at[:, pl.ds(HIDDEN, HIDDEN)], w_sem.at[1]),
        pltpu.make_async_copy(wd_hbm.at[0], wd, w_sem.at[2]),
    ]
    for copy in weights:
        copy.start()

    barrier = pltpu.get_barrier_semaphore()
    pl.semaphore_signal(barrier, inc=1, device_id=sibling, device_id_type=MESH)
    for axis in range(3):
        for delta in (2, 1, 3):
            pl.semaphore_signal(barrier, inc=1, device_id=peer(axis, delta), device_id_type=MESH)

    lane = lax.broadcasted_iota(jnp.int32, (4, LANE), 1)

    def own_rows(c):
        at = pl.multiple_of(c * HALF, LANE)
        return jnp.concatenate(
            [hs[s, :, pl.ds(at, HALF)].astype(F32) for s in range(STEPS)], axis=0
        )

    tables = []
    for s in range(STEPS):
        total = jnp.zeros((4, LANE), F32)
        for k in range(8):
            total += jnp.where(
                lane == routes[s, :, k : k + 1], gates[s, :, k : k + 1].astype(F32), 0.0
            )
        tables.append(total)
    table = jnp.concatenate(tables, axis=0)

    zero_send[:, pl.ds(0, HALF)] = own_rows(1 - core)
    zero_send[:, pl.ds(HALF, LANE)] = table
    h[...] = jnp.zeros_like(h)
    pl.semaphore_wait(barrier, 10)
    swap = pltpu.make_async_remote_copy(
        src_ref=zero_send, dst_ref=zero_recv, send_sem=e_send.at[0], recv_sem=e_recv.at[0],
        device_id=sibling, device_id_type=MESH,
    )
    swap.start()
    base = pl.multiple_of(core * HALF_T, LANE)
    mine = jnp.concatenate([own_rows(core), table], axis=1)
    first = core == 0
    swap.wait()
    theirs = zero_recv[...]
    low, high = jnp.where(first, mine, theirs), jnp.where(first, theirs, mine)
    for s in range(STEPS):
        tile = jnp.concatenate([low[4 * s : 4 * s + 4], high[4 * s : 4 * s + 4]], axis=0)
        X[s, me[0], me[1], me[2], :, pl.ds(base, HALF_T)] = tile.astype(BF16)

    def spread(q, places):
        index = [None] * 3
        for axis, j in zip(PARTS[q[0]][q[1]][2], places):
            if j is None:
                j = pl.ds(0, 4)
            index[axis] = j if isinstance(j, pl.Slice) else pl.ds(j, 1)
        return (q[0],) + tuple(index)

    def block(q, places, c, units):
        at = pl.multiple_of(c * HALF_T + units[0] * LANE, LANE)
        return spread(q, places) + (pl.ds(0, TILE), pl.ds(at, units[1] * LANE))

    def axis_of(q, n):
        return PARTS[q[0]][q[1]][2][n]

    def near(q, n, offset):
        return place(axis_of(q, n), offset)

    def index_of(q, count, k):
        return (q[0] * N_PARTS + q[1]) * count + k

    def remote(src, dst, sends, send, recvs, recv, device):
        return pltpu.make_async_remote_copy(
            src_ref=src, dst_ref=dst, send_sem=sends.at[send], recv_sem=recvs.at[recv],
            device_id=device, device_id_type=MESH,
        )

    def wait_for(ref, sem):
        pltpu.make_async_copy(ref, ref, sem).wait()

    def sized(q, places, table):
        return X.at[block(q, places, core, part_units(q, table))]

    def tiles(q, count, table):
        return sized(q, (pl.ds(0, count), 0, 0), table)

    def lines(q, count, table):
        return sized(q, (None, pl.ds(0, count), 0), table)

    def planes(q, count, table):
        return sized(q, (None, None, pl.ds(0, count)), table)

    def some(q, stage, units):
        return X.at[block(q, ((None, None, 0) if stage == 3 else (None, 0, 0)), core, units)]

    def gather_copy(q, places, units, send, recv, device):
        ref = X.at[block(q, places, core, units)]
        return remote(ref, ref, g_send, index_of(q, G_SENDS, send), g_recv, index_of(q, G_RECVS, recv), device)

    def sent(q, send, ref):
        wait_for(ref, g_send.at[index_of(q, G_SENDS, send)])

    def came(q, recv, ref):
        wait_for(ref, g_recv.at[index_of(q, G_RECVS, recv)])

    def ring(q, stage, units, offset, to, recv):
        places = (
            (None, near(q, 1, offset), near(q, 2, 0)) if stage == 2 else (None, None, near(q, 2, offset))
        )
        gather_copy(q, places, units, stage - 1, recv, peer(axis_of(q, stage - 1), to)).start()

    def passed(q, offset, recv):
        ref = X.at[block(q, (None, None, near(q, 2, offset)), core, part_units(q, False))]
        remote(
            ref, ref, g_send, index_of(q, G_SENDS, 3), g_recv, index_of(q, G_RECVS, recv), sibling
        ).start()

    def multiply(q, offsets, c):
        units = part_units(q, False)
        rows = [
            X[block(q, (None, None, near(q, 2, o)), c, units)].reshape(16 * TILE, units[1] * LANE)
            for o in offsets
        ]
        rows = rows[0] if len(rows) == 1 else jnp.concatenate(rows, axis=0)
        at = pl.multiple_of(c * HALF + units[0] * LANE, LANE)
        found = jnp.dot(rows, wgu[pl.ds(at, units[1] * LANE), :], preferred_element_type=F32)
        for i, o in enumerate(offsets):
            where = spread(q, (None, None, near(q, 2, o)))
            h[where] += found[i * 16 * TILE : (i + 1) * 16 * TILE].reshape(h[where].shape)

    def each(step):
        def over(s):
            for p in parts:
                step((s, p))
        return over

    @each
    def g1(q):
        for d in (2, 1, 3):
            places = tuple(near(q, i, 0) for i in range(3))
            gather_copy(q, places, part_units(q, True), 0, 0, peer(axis_of(q, 0), d)).start()

    @each
    def g2(q):
        came(q, 0, tiles(q, 3, True))
        a, b = halves(q, True)
        ring(q, 2, a, 0, 1, 1)
        ring(q, 2, b, 0, 3, 2)
        ring(q, 2, b, 0, 1, 3)
        ring(q, 2, a, 0, 3, 3)

    @each
    def g3(q):
        a, b = halves(q, True)
        came(q, 1, some(q, 2, a))
        ring(q, 2, a, 3, 1, 3)
        came(q, 2, some(q, 2, b))
        ring(q, 2, b, 1, 3, 3)

    @each
    def g4(q):
        came(q, 3, lines(q, 2, True))
        a, b = halves(q, True)
        ring(q, 3, a, 0, 1, 4)
        ring(q, 3, b, 0, 3, 5)
        ring(q, 3, b, 0, 1, 6)
        ring(q, 3, a, 0, 3, 6)
        passed(q, 0, 8)

    @each
    def g5(q):
        a, b = halves(q, True)
        came(q, 4, some(q, 3, a))
        ring(q, 3, a, 3, 1, 7)
        came(q, 5, some(q, 3, b))
        ring(q, 3, b, 1, 3, 7)

    @each
    def g6(q):
        came(q, 6, planes(q, 1, True))
        passed(q, 3, 9)
        passed(q, 1, 10)

    @each
    def g7(q):
        came(q, 7, planes(q, 1, True))
        passed(q, 2, 11)

    @each
    def c0(q):
        multiply(q, (0,), core)

    @each
    def c1(q):
        came(q, 8, planes(q, 1, False))
        multiply(q, (0,), 1 - core)

    @each
    def c2(q):
        multiply(q, (3, 1), core)

    @each
    def c3(q):
        came(q, 9, planes(q, 1, False))
        came(q, 10, planes(q, 1, False))
        multiply(q, (3, 1), 1 - core)

    @each
    def c4(q):
        multiply(q, (2,), core)

    @each
    def c5(q):
        came(q, 11, planes(q, 1, False))
        multiply(q, (2,), 1 - core)

    chosen = (lax.broadcasted_iota(jnp.int32, (LANE, HIDDEN), 0) == ep // 4).astype(BF16)
    table_at = pl.multiple_of(base + HALF, LANE)

    def activate(s):
        def one(i, carry):
            rows = X[s, i, :, :, :, pl.ds(table_at, LANE)].reshape(16 * TILE, LANE)
            scaled = jnp.dot(rows, chosen, preferred_element_type=F32)
            both = h[s, i].reshape(16 * TILE, 2 * HIDDEN)
            gate, up = both[:, :HIDDEN], both[:, HIDDEN:]
            value = gate / (1.0 + jnp.exp(-gate)) * up * scaled
            act[s, i] = value.astype(BF16).reshape(4, 4, TILE, HIDDEN)
            return carry

        lax.fori_loop(0, 4, one, 0)
        for p in parts:
            q = (s, p)
            sent(q, 0, tiles(q, 3, True))
            sent(q, 1, lines(q, 3, True))
            sent(q, 2, planes(q, 3, True))
            sent(q, 3, planes(q, 4, False))

    def down(q, offset, c):
        first_unit, count = part_units(q, False)
        rows = act[spread(q, (None, None, near(q, 2, offset)))].reshape(16 * TILE, HIDDEN)
        at = pl.multiple_of(c * HALF + first_unit * LANE, LANE)
        return jnp.dot(rows, wd[:, pl.ds(at, count * LANE)], preferred_element_type=F32)

    def cross_places(q, offset, c):
        units = part_units(q, False)
        places = (None, None, near(q, 2, offset))
        to = spread(q, places) + (pl.ds(0, TILE), pl.ds(units[0] * LANE, units[1] * LANE))
        return block(q, places, c, units), to

    def scatter_copy(q, src, dst, send, recv, device):
        remote(
            src, dst, b_send, index_of(q, B_SENDS, send), b_recv, index_of(q, B_RECVS, recv), device
        ).start()

    def left_off(q, send, ref):
        wait_for(ref, b_send.at[index_of(q, B_SENDS, send)])

    def landed(q, recv, ref):
        wait_for(ref, b_recv.at[index_of(q, B_RECVS, recv)])

    def theirs_out(s, offset):
        for p in parts:
            q = (s, p)
            where, to = cross_places(q, offset, 1 - core)
            X[where] = down(q, offset, 1 - core).astype(BF16).reshape(X[where].shape)
            scatter_copy(q, X.at[where], R0.at[to], 0, offset, sibling)

    def mine_out(s, offset):
        for p in parts:
            q = (s, p)
            where, to = cross_places(q, offset, core)
            found = down(q, offset, core)
            landed(q, offset, planes(q, 1, False))
            X[where] = (found.reshape(X[where].shape) + R0[to].astype(F32)).astype(BF16)
            if offset == 2:
                a, b = halves(q, False)
                ring_out(q, 3, 2, a, 0, 1, 4)
                ring_out(q, 3, 2, b, 0, 3, 5)

    def span(q, units):
        return pl.ds((units[0] - part_units(q, False)[0]) * LANE, units[1] * LANE)

    every = slice(None)

    def ring_out(q, stage, offset, units, slot, to, recv):
        places = (
            (None, near(q, 1, offset), near(q, 2, 0)) if stage == 2 else (None, None, near(q, 2, offset))
        )
        buffer = (R2 if stage == 2 else R3)[q]
        dst = buffer.at[slot, every, every, every, every, span(q, units)]
        scatter_copy(
            q, X.at[block(q, places, core, units)], dst, 1 if stage == 3 else 2, recv,
            peer(axis_of(q, stage - 1), to),
        )

    def accumulate(where, terms):
        total = X[where].astype(F32)
        for term in terms:
            total += term.astype(F32)
        X[where] = total.astype(BF16)

    @each
    def r1(q):
        a, b = halves(q, False)
        ring_out(q, 3, 1, b, 1, 1, 6)
        ring_out(q, 3, 3, a, 2, 3, 6)

    def relay(q):
        a, b = halves(q, False)
        for units, offset, recv in ((a, 1, 4), (b, 3, 5)):
            landed(q, recv, some(q, 3, units))
            term = R3[q][0, :, :, :, :, span(q, units)]
            accumulate(block(q, (None, None, near(q, 2, offset)), core, units), (term,))

    @each
    def r2(q):
        a, b = halves(q, False)
        relay(q)
        ring_out(q, 3, 1, a, 1, 1, 6)
        ring_out(q, 3, 3, b, 2, 3, 6)

    @each
    def r3(q):
        landed(q, 6, planes(q, 2, False))
        where = block(q, (None, None, near(q, 2, 0)), core, part_units(q, False))
        accumulate(where, (R3[q][1], R3[q][2]))
        a, b = halves(q, False)
        ring_out(q, 2, 2, a, 0, 1, 7)
        ring_out(q, 2, 2, b, 0, 3, 8)
        ring_out(q, 2, 1, b, 1, 1, 9)
        ring_out(q, 2, 3, a, 2, 3, 9)

    def line_index(q, line):
        return spread(q, (None, near(q, 1, line), 0))[1:]

    def r2_lines(s):
        for p in parts:
            relay((s, p))
        for line in (2, 1, 3, 0):
            for p in parts:
                q = (s, p)
                for units, offset, slot in zip(halves(q, False), (1, 3), (1, 2)):
                    src = X.at[block(q, (None, near(q, 1, line), near(q, 2, offset)), core, units)]
                    dst = R3[q].at[(slot,) + line_index(q, line) + (every, span(q, units))]
                    scatter_copy(q, src, dst, 1, 11 + line, peer(axis_of(q, 2), offset))

    def r3_lines(s):
        for p in parts:
            landed((s, p), 6, planes((s, p), 1, False))
        for line in (2, 1, 3, 0):
            for p in parts:
                q = (s, p)
                landed(q, 11 + line, lines(q, 1, False))
                where = block(q, (None, near(q, 1, line), near(q, 2, 0)), core, part_units(q, False))
                accumulate(where, tuple(R3[q][(slot,) + line_index(q, line)] for slot in (1, 2)))
                if line:
                    scatter_copy(q, X.at[where], R2[q].at[line - 1], 2, 9, peer(axis_of(q, 1), line))

    @each
    def r4(q):
        a, b = halves(q, False)
        for units, offset, slot, recv in ((a, 1, 1, 7), (b, 3, 2, 8)):
            landed(q, recv, some(q, 2, units))
            term = R2[q][0, :, :, :, :, span(q, units)]
            accumulate(block(q, (None, near(q, 1, offset), near(q, 2, 0)), core, units), (term,))
            ring_out(q, 2, offset, units, slot, offset, 9)

    @each
    def r5(q):
        units = part_units(q, False)
        if q[0] == STEPS - 1:
            landed(q, 9, lines(q, 3, False))
            terms = (R2[q][0], R2[q][1], R2[q][2])
        else:
            landed(q, 9, lines(q, 2, False))
            terms = (R2[q][1], R2[q][2])
        accumulate(block(q, (None, near(q, 1, 0), near(q, 2, 0)), core, units), terms)
        for d in (2, 1, 3):
            places = (near(q, 0, d), near(q, 1, 0), near(q, 2, 0))
            src = X.at[block(q, places, core, units)]
            scatter_copy(q, src, R1[q].at[d - 1], 3, 10, peer(axis_of(q, 0), d))

    def wait_weights(i):
        weights[i].wait()

    g1(0)
    g1(1)
    g2(0)
    g2(1)
    g3(0)
    g3(1)
    g4(0)
    wait_weights(0); wait_weights(1)
    c0(0)
    c1(0)
    g5(0)
    g4(1)
    c0(1)
    g6(0)
    c2(0)
    c3(0)
    g7(0)
    c4(0)
    c5(0)
    activate(0)
    wait_weights(2)
    theirs_out(0, 2)
    g5(1)
    mine_out(0, 2)
    theirs_out(0, 1)
    theirs_out(0, 3)
    mine_out(0, 1)
    mine_out(0, 3)
    r1(0)
    theirs_out(0, 0)
    c1(1)
    mine_out(0, 0)
    g6(1)
    c2(1)
    c3(1)
    g7(1)
    c4(1)
    c5(1)
    activate(1)
    theirs_out(1, 2)
    r2(0)
    mine_out(1, 2)
    theirs_out(1, 1)
    theirs_out(1, 3)
    mine_out(1, 1)
    mine_out(1, 3)
    r1(1)
    theirs_out(1, 0)
    mine_out(1, 0)
    r2_lines(1)
    r3(0)
    r4(0)
    r3_lines(1)
    r5(0)
    r5(1)

    kept, given = [], []
    for s in range(STEPS):
        pieces = []
        for p in parts:
            q = (s, p)
            units = part_units(q, False)
            where = block(q, tuple(near(q, i, 0) for i in range(3)), core, units)
            total = X[where].astype(F32).reshape(TILE, units[1] * LANE)
            landed(q, 10, tiles(q, 3, False))
            for d in (1, 2, 3):
                total += R1[q][d - 1].astype(F32).reshape(TILE, units[1] * LANE)
            pieces.append(total)
        tile = jnp.concatenate(pieces, axis=1)
        kept.append(jnp.where(first, tile[:4], tile[4:]))
        given.append(jnp.where(first, tile[4:], tile[:4]))
    last_send[...] = jnp.concatenate(given, axis=0)
    swap_back = pltpu.make_async_remote_copy(
        src_ref=last_send, dst_ref=last_recv, send_sem=e_send.at[1], recv_sem=e_recv.at[1],
        device_id=sibling, device_id_type=MESH,
    )
    swap_back.start()
    at = pl.multiple_of(core * HALF, LANE)
    for s in range(STEPS):
        out[s, :, pl.ds(at, HALF)] = kept[s].astype(BF16)
    for q in PAIRS:
        left_off(q, 0, planes(q, 4, False))
        left_off(q, 1, planes(q, 3, False))
        left_off(q, 2, lines(q, 3, False))
        left_off(q, 3, tiles(q, 3, False))
    swap_back.wait()
    other = last_recv[...].astype(BF16)
    at = pl.multiple_of((1 - core) * HALF, LANE)
    for s in range(STEPS):
        out[s, :, pl.ds(at, HALF)] = other[4 * s : 4 * s + 4]


def scatter_shapes():
    shapes = []
    for stage in (3, 2, 1):
        for s, p in PAIRS:
            _, count, order = PARTS[s][p]
            dims = tuple(4 if a in order[: stage - 1] else 1 for a in range(3))
            shapes.append(pltpu.VMEM((3,) + dims + (TILE, count * LANE), BF16))
    return shapes


def body(hidden_states, expert_routes, route_gates, gate_weights, up_weights, down_weights):
    width = hidden_states.shape[2]
    vmem = pl.BlockSpec(memory_space=pltpu.VMEM)
    hbm = pl.BlockSpec(memory_space=pl.ANY)
    pairs = len(PAIRS)
    copies = [
        pltpu.SemaphoreType.DMA((count,))
        for count in (3, 2, 2, *(pairs * k for k in (G_SENDS, G_RECVS, B_SENDS, B_RECVS)))
    ]
    return pl.pallas_call(
        kernel,
        out_shape=jax.ShapeDtypeStruct(hidden_states.shape, BF16),
        in_specs=[vmem, vmem, vmem, hbm, hbm, hbm],
        out_specs=vmem,
        scratch_shapes=[
            pltpu.VMEM((STEPS, 4, 4, 4, TILE, 2 * HALF_T), BF16),
            pltpu.VMEM((width, 2 * HIDDEN), BF16),
            pltpu.VMEM((HIDDEN, width), BF16),
            pltpu.VMEM((STEPS, 4, 4, 4, TILE, 2 * HIDDEN), F32),
            pltpu.VMEM((STEPS, 4, 4, 4, TILE, HIDDEN), BF16),
            pltpu.VMEM((8, HALF_T), F32),
            pltpu.VMEM((8, HALF_T), F32),
            pltpu.VMEM((8, HALF), F32),
            pltpu.VMEM((8, HALF), F32),
            pltpu.VMEM((STEPS, 4, 4, 4, TILE, HALF), BF16),
            *scatter_shapes(),
            *copies,
        ],
        compiler_params=pltpu.CompilerParams(
            collective_id=0, has_side_effects=True, vmem_limit_bytes=60 * 1024 * 1024
        ),
        cost_estimate=pl.CostEstimate(
            flops=11_300_000_000, bytes_accessed=12_000_000, transcendentals=262144
        ),
    )(hidden_states, expert_routes, route_gates, gate_weights, up_weights, down_weights)


def solution(mesh):
    return jax.shard_map(
        body,
        mesh=mesh,
        in_specs=(
            P(None, ("grp", "ep"), None),
            P(None, ("grp", "ep"), None),
            P(None, ("grp", "ep"), None),
            P("ep", None, "grp"),
            P("ep", None, "grp"),
            P("ep", "grp", None),
        ),
        out_specs=P(None, ("grp", "ep"), None),
        check_vma=False,
    )
```

```python
import jax
import jax.numpy as jnp
from jax import lax
from jax.experimental import pallas as pl
from jax.experimental.pallas import tpu as pltpu
from jax.sharding import PartitionSpec as P

LANE = 128
TILE = 8
UNITS = 28
HALF = UNITS * LANE
HALF_T = HALF + LANE
HIDDEN = 256
STEPS = 2
MESH = pl.DeviceIdType.MESH
F32 = jnp.float32
BF16 = jnp.bfloat16

PARTS = (
    ((0, 10, (2, 1, 0)), (10, 9, (0, 2, 1)), (19, 9, (1, 0, 2))),
    ((0, 10, (0, 2, 1)), (10, 9, (1, 0, 2)), (19, 9, (2, 1, 0))),
)
TABLE_PART = 2
N_PARTS = 3
G_SENDS, G_RECVS, B_SENDS, B_RECVS = 4, 12, 4, 15
PAIRS = tuple((s, p) for s in range(STEPS) for p in range(N_PARTS))


def part_units(q, table):
    first, count, _ = PARTS[q[0]][q[1]]
    return first, count + (1 if table and q[1] == TABLE_PART else 0)


def halves(q, table):
    first, count = part_units(q, table)
    left = (count + 1 - q[0] % 2) // 2
    return (first, left), (first + left, count - left)


def kernel(
    hs, routes, gates, wg_hbm, wu_hbm, wd_hbm,
    out,
    X, wgu, wd, h, act, zero_send, zero_recv, last_send, last_recv, R0,
    *rest,
):
    n = len(PAIRS)
    R3, R2, R1 = (dict(zip(PAIRS, rest[i * n : (i + 1) * n])) for i in range(3))
    w_sem, e_send, e_recv, g_send, g_recv, b_send, b_recv = rest[3 * n :]
    core = lax.axis_index("grp")
    ep = lax.axis_index("ep")
    me = (ep // 16, (ep // 4) % 4, ep % 4)
    sibling = (1 - core, ep)
    scale = (16, 4, 1)
    parts = range(N_PARTS)

    spots = [[lax.rem(me[axis] + d, 4) for d in range(4)] for axis in range(3)]
    peers = [
        [(core, ep + (spots[axis][d] - me[axis]) * scale[axis]) for d in range(4)] for axis in range(3)
    ]

    def place(axis, delta):
        return spots[axis][delta % 4]

    def peer(axis, delta):
        return peers[axis][delta]

    weights = [
        pltpu.make_async_copy(wg_hbm.at[0], wgu.at[:, pl.ds(0, HIDDEN)], w_sem.at[0]),
        pltpu.make_async_copy(wu_hbm.at[0], wgu.at[:, pl.ds(HIDDEN, HIDDEN)], w_sem.at[1]),
        pltpu.make_async_copy(wd_hbm.at[0], wd, w_sem.at[2]),
    ]
    for copy in weights:
        copy.start()

    barrier = pltpu.get_barrier_semaphore()
    pl.semaphore_signal(barrier, inc=1, device_id=sibling, device_id_type=MESH)
    for axis in range(3):
        for delta in (2, 1, 3):
            pl.semaphore_signal(barrier, inc=1, device_id=peer(axis, delta), device_id_type=MESH)

    lane = lax.broadcasted_iota(jnp.int32, (4, LANE), 1)

    def own_rows(c):
        at = pl.multiple_of(c * HALF, LANE)
        return jnp.concatenate(
            [hs[s, :, pl.ds(at, HALF)].astype(F32) for s in range(STEPS)], axis=0
        )

    tables = []
    for s in range(STEPS):
        total = jnp.zeros((4, LANE), F32)
        for k in range(8):
            total += jnp.where(
                lane == routes[s, :, k : k + 1], gates[s, :, k : k + 1].astype(F32), 0.0
            )
        tables.append(total)
    table = jnp.concatenate(tables, axis=0)

    zero_send[:, pl.ds(0, HALF)] = own_rows(1 - core)
    zero_send[:, pl.ds(HALF, LANE)] = table
    h[...] = jnp.zeros_like(h)
    pl.semaphore_wait(barrier, 10)
    swap = pltpu.make_async_remote_copy(
        src_ref=zero_send, dst_ref=zero_recv, send_sem=e_send.at[0], recv_sem=e_recv.at[0],
        device_id=sibling, device_id_type=MESH,
    )
    swap.start()
    base = pl.multiple_of(core * HALF_T, LANE)
    mine = jnp.concatenate([own_rows(core), table], axis=1)
    first = core == 0
    swap.wait()
    theirs = zero_recv[...]
    low, high = jnp.where(first, mine, theirs), jnp.where(first, theirs, mine)
    for s in range(STEPS):
        tile = jnp.concatenate([low[4 * s : 4 * s + 4], high[4 * s : 4 * s + 4]], axis=0)
        X[s, me[0], me[1], me[2], :, pl.ds(base, HALF_T)] = tile.astype(BF16)

    def spread(q, places):
        index = [None] * 3
        for axis, j in zip(PARTS[q[0]][q[1]][2], places):
            if j is None:
                j = pl.ds(0, 4)
            index[axis] = j if isinstance(j, pl.Slice) else pl.ds(j, 1)
        return (q[0],) + tuple(index)

    def block(q, places, c, units):
        at = pl.multiple_of(c * HALF_T + units[0] * LANE, LANE)
        return spread(q, places) + (pl.ds(0, TILE), pl.ds(at, units[1] * LANE))

    def axis_of(q, n):
        return PARTS[q[0]][q[1]][2][n]

    def near(q, n, offset):
        return place(axis_of(q, n), offset)

    def index_of(q, count, k):
        return (q[0] * N_PARTS + q[1]) * count + k

    def remote(src, dst, sends, send, recvs, recv, device):
        return pltpu.make_async_remote_copy(
            src_ref=src, dst_ref=dst, send_sem=sends.at[send], recv_sem=recvs.at[recv],
            device_id=device, device_id_type=MESH,
        )

    def wait_for(ref, sem):
        pltpu.make_async_copy(ref, ref, sem).wait()

    def sized(q, places, table):
        return X.at[block(q, places, core, part_units(q, table))]

    def tiles(q, count, table):
        return sized(q, (pl.ds(0, count), 0, 0), table)

    def lines(q, count, table):
        return sized(q, (None, pl.ds(0, count), 0), table)

    def planes(q, count, table):
        return sized(q, (None, None, pl.ds(0, count)), table)

    def some(q, stage, units):
        return X.at[block(q, ((None, None, 0) if stage == 3 else (None, 0, 0)), core, units)]

    def gather_copy(q, places, units, send, recv, device):
        ref = X.at[block(q, places, core, units)]
        return remote(ref, ref, g_send, index_of(q, G_SENDS, send), g_recv, index_of(q, G_RECVS, recv), device)

    def sent(q, send, ref):
        wait_for(ref, g_send.at[index_of(q, G_SENDS, send)])

    def came(q, recv, ref):
        wait_for(ref, g_recv.at[index_of(q, G_RECVS, recv)])

    def ring(q, stage, units, offset, to, recv):
        places = (
            (None, near(q, 1, offset), near(q, 2, 0)) if stage == 2 else (None, None, near(q, 2, offset))
        )
        gather_copy(q, places, units, stage - 1, recv, peer(axis_of(q, stage - 1), to)).start()

    def passed(q, offset, recv):
        ref = X.at[block(q, (None, None, near(q, 2, offset)), core, part_units(q, False))]
        remote(
            ref, ref, g_send, index_of(q, G_SENDS, 3), g_recv, index_of(q, G_RECVS, recv), sibling
        ).start()

    def multiply(q, offsets, c):
        units = part_units(q, False)
        rows = [
            X[block(q, (None, None, near(q, 2, o)), c, units)].reshape(16 * TILE, units[1] * LANE)
            for o in offsets
        ]
        rows = rows[0] if len(rows) == 1 else jnp.concatenate(rows, axis=0)
        at = pl.multiple_of(c * HALF + units[0] * LANE, LANE)
        found = jnp.dot(rows, wgu[pl.ds(at, units[1] * LANE), :], preferred_element_type=F32)
        for i, o in enumerate(offsets):
            where = spread(q, (None, None, near(q, 2, o)))
            h[where] += found[i * 16 * TILE : (i + 1) * 16 * TILE].reshape(h[where].shape)

    def each(step):
        def over(s):
            for p in parts:
                step((s, p))
        return over

    @each
    def g1(q):
        for d in (2, 1, 3):
            places = tuple(near(q, i, 0) for i in range(3))
            gather_copy(q, places, part_units(q, True), 0, 0, peer(axis_of(q, 0), d)).start()

    @each
    def g2(q):
        came(q, 0, tiles(q, 3, True))
        a, b = halves(q, True)
        ring(q, 2, a, 0, 1, 1)
        ring(q, 2, b, 0, 3, 2)
        ring(q, 2, b, 0, 1, 3)
        ring(q, 2, a, 0, 3, 3)

    @each
    def g3(q):
        a, b = halves(q, True)
        came(q, 1, some(q, 2, a))
        ring(q, 2, a, 3, 1, 3)
        came(q, 2, some(q, 2, b))
        ring(q, 2, b, 1, 3, 3)

    @each
    def g4(q):
        came(q, 3, lines(q, 2, True))
        a, b = halves(q, True)
        ring(q, 3, a, 0, 1, 4)
        ring(q, 3, b, 0, 3, 5)
        ring(q, 3, b, 0, 1, 6)
        ring(q, 3, a, 0, 3, 6)
        passed(q, 0, 8)

    @each
    def g5(q):
        a, b = halves(q, True)
        came(q, 4, some(q, 3, a))
        ring(q, 3, a, 3, 1, 7)
        came(q, 5, some(q, 3, b))
        ring(q, 3, b, 1, 3, 7)

    @each
    def g6(q):
        came(q, 6, planes(q, 1, True))
        passed(q, 3, 9)
        passed(q, 1, 10)

    @each
    def g7(q):
        came(q, 7, planes(q, 1, True))
        passed(q, 2, 11)

    @each
    def c0(q):
        multiply(q, (0,), core)

    @each
    def c1(q):
        came(q, 8, planes(q, 1, False))
        multiply(q, (0,), 1 - core)

    @each
    def c2(q):
        multiply(q, (3, 1), core)

    @each
    def c3(q):
        came(q, 9, planes(q, 1, False))
        came(q, 10, planes(q, 1, False))
        multiply(q, (3, 1), 1 - core)

    @each
    def c4(q):
        multiply(q, (2,), core)

    @each
    def c5(q):
        came(q, 11, planes(q, 1, False))
        multiply(q, (2,), 1 - core)

    chosen = (lax.broadcasted_iota(jnp.int32, (LANE, HIDDEN), 0) == ep // 4).astype(BF16)
    table_at = pl.multiple_of(base + HALF, LANE)

    def activate(s):
        def one(i, carry):
            rows = X[s, i, :, :, :, pl.ds(table_at, LANE)].reshape(16 * TILE, LANE)
            scaled = jnp.dot(rows, chosen, preferred_element_type=F32)
            both = h[s, i].reshape(16 * TILE, 2 * HIDDEN)
            gate, up = both[:, :HIDDEN], both[:, HIDDEN:]
            value = gate / (1.0 + jnp.exp(-gate)) * up * scaled
            act[s, i] = value.astype(BF16).reshape(4, 4, TILE, HIDDEN)
            return carry

        lax.fori_loop(0, 4, one, 0)
        for p in parts:
            q = (s, p)
            sent(q, 0, tiles(q, 3, True))
            sent(q, 1, lines(q, 3, True))
            sent(q, 2, planes(q, 3, True))
            sent(q, 3, planes(q, 4, False))

    def down(q, offset, c):
        first_unit, count = part_units(q, False)
        rows = act[spread(q, (None, None, near(q, 2, offset)))].reshape(16 * TILE, HIDDEN)
        at = pl.multiple_of(c * HALF + first_unit * LANE, LANE)
        return jnp.dot(rows, wd[:, pl.ds(at, count * LANE)], preferred_element_type=F32)

    def cross_places(q, offset, c):
        units = part_units(q, False)
        places = (None, None, near(q, 2, offset))
        to = spread(q, places) + (pl.ds(0, TILE), pl.ds(units[0] * LANE, units[1] * LANE))
        return block(q, places, c, units), to

    def scatter_copy(q, src, dst, send, recv, device):
        remote(
            src, dst, b_send, index_of(q, B_SENDS, send), b_recv, index_of(q, B_RECVS, recv), device
        ).start()

    def left_off(q, send, ref):
        wait_for(ref, b_send.at[index_of(q, B_SENDS, send)])

    def landed(q, recv, ref):
        wait_for(ref, b_recv.at[index_of(q, B_RECVS, recv)])

    def theirs_out(s, offset):
        for p in parts:
            q = (s, p)
            where, to = cross_places(q, offset, 1 - core)
            X[where] = down(q, offset, 1 - core).astype(BF16).reshape(X[where].shape)
            scatter_copy(q, X.at[where], R0.at[to], 0, offset, sibling)

    def mine_out(s, offset):
        for p in parts:
            q = (s, p)
            where, to = cross_places(q, offset, core)
            found = down(q, offset, core)
            landed(q, offset, planes(q, 1, False))
            X[where] = (found.reshape(X[where].shape) + R0[to].astype(F32)).astype(BF16)
            if offset == 2:
                a, b = halves(q, False)
                ring_out(q, 3, 2, a, 0, 1, 4)
                ring_out(q, 3, 2, b, 0, 3, 5)

    def span(q, units):
        return pl.ds((units[0] - part_units(q, False)[0]) * LANE, units[1] * LANE)

    every = slice(None)

    def ring_out(q, stage, offset, units, slot, to, recv):
        places = (
            (None, near(q, 1, offset), near(q, 2, 0)) if stage == 2 else (None, None, near(q, 2, offset))
        )
        buffer = (R2 if stage == 2 else R3)[q]
        dst = buffer.at[slot, every, every, every, every, span(q, units)]
        scatter_copy(
            q, X.at[block(q, places, core, units)], dst, 1 if stage == 3 else 2, recv,
            peer(axis_of(q, stage - 1), to),
        )

    def accumulate(where, terms):
        total = X[where].astype(F32)
        for term in terms:
            total += term.astype(F32)
        X[where] = total.astype(BF16)

    @each
    def r1(q):
        a, b = halves(q, False)
        ring_out(q, 3, 1, b, 1, 1, 6)
        ring_out(q, 3, 3, a, 2, 3, 6)

    def relay(q):
        a, b = halves(q, False)
        for units, offset, recv in ((a, 1, 4), (b, 3, 5)):
            landed(q, recv, some(q, 3, units))
            term = R3[q][0, :, :, :, :, span(q, units)]
            accumulate(block(q, (None, None, near(q, 2, offset)), core, units), (term,))

    @each
    def r2(q):
        a, b = halves(q, False)
        relay(q)
        ring_out(q, 3, 1, a, 1, 1, 6)
        ring_out(q, 3, 3, b, 2, 3, 6)

    @each
    def r3(q):
        landed(q, 6, planes(q, 2, False))
        where = block(q, (None, None, near(q, 2, 0)), core, part_units(q, False))
        accumulate(where, (R3[q][1], R3[q][2]))
        a, b = halves(q, False)
        ring_out(q, 2, 2, a, 0, 1, 7)
        ring_out(q, 2, 2, b, 0, 3, 8)
        ring_out(q, 2, 1, b, 1, 1, 9)
        ring_out(q, 2, 3, a, 2, 3, 9)

    def line_index(q, line):
        return spread(q, (None, near(q, 1, line), 0))[1:]

    def r2_lines(s):
        for p in parts:
            relay((s, p))
        for line in (2, 1, 3, 0):
            for p in parts:
                q = (s, p)
                for units, offset, slot in zip(halves(q, False), (1, 3), (1, 2)):
                    src = X.at[block(q, (None, near(q, 1, line), near(q, 2, offset)), core, units)]
                    dst = R3[q].at[(slot,) + line_index(q, line) + (every, span(q, units))]
                    scatter_copy(q, src, dst, 1, 11 + line, peer(axis_of(q, 2), offset))

    def r3_lines(s):
        for p in parts:
            landed((s, p), 6, planes((s, p), 1, False))
        for line in (2, 1, 3, 0):
            for p in parts:
                q = (s, p)
                landed(q, 11 + line, lines(q, 1, False))
                where = block(q, (None, near(q, 1, line), near(q, 2, 0)), core, part_units(q, False))
                accumulate(where, tuple(R3[q][(slot,) + line_index(q, line)] for slot in (1, 2)))
                if line:
                    scatter_copy(q, X.at[where], R2[q].at[line - 1], 2, 9, peer(axis_of(q, 1), line))

    @each
    def r4(q):
        a, b = halves(q, False)
        for units, offset, slot, recv in ((a, 1, 1, 7), (b, 3, 2, 8)):
            landed(q, recv, some(q, 2, units))
            term = R2[q][0, :, :, :, :, span(q, units)]
            accumulate(block(q, (None, near(q, 1, offset), near(q, 2, 0)), core, units), (term,))
            ring_out(q, 2, offset, units, slot, offset, 9)

    @each
    def r5(q):
        units = part_units(q, False)
        if q[0] == STEPS - 1:
            landed(q, 9, lines(q, 3, False))
            terms = (R2[q][0], R2[q][1], R2[q][2])
        else:
            landed(q, 9, lines(q, 2, False))
            terms = (R2[q][1], R2[q][2])
        accumulate(block(q, (None, near(q, 1, 0), near(q, 2, 0)), core, units), terms)
        for d in (2, 1, 3):
            places = (near(q, 0, d), near(q, 1, 0), near(q, 2, 0))
            src = X.at[block(q, places, core, units)]
            scatter_copy(q, src, R1[q].at[d - 1], 3, 10, peer(axis_of(q, 0), d))

    def swap_back(s):
        return pltpu.make_async_remote_copy(
            src_ref=last_send.at[s], dst_ref=last_recv.at[s], send_sem=e_send.at[1 + s],
            recv_sem=e_recv.at[1 + s], device_id=sibling, device_id_type=MESH,
        )

    def finish(s):
        pieces = []
        for p in parts:
            q = (s, p)
            units = part_units(q, False)
            where = block(q, tuple(near(q, i, 0) for i in range(3)), core, units)
            total = X[where].astype(F32).reshape(TILE, units[1] * LANE)
            landed(q, 10, tiles(q, 3, False))
            for d in (1, 2, 3):
                total += R1[q][d - 1].astype(F32).reshape(TILE, units[1] * LANE)
            pieces.append(total)
        tile = jnp.concatenate(pieces, axis=1)
        last_send[s] = jnp.where(first, tile[4:], tile[:4])
        swap_back(s).start()
        at = pl.multiple_of(core * HALF, LANE)
        out[s, :, pl.ds(at, HALF)] = jnp.where(first, tile[:4], tile[4:]).astype(BF16)

    def wait_weights(i):
        weights[i].wait()

    g1(0)
    g1(1)
    g2(0)
    g2(1)
    g3(0)
    g3(1)
    g4(0)
    wait_weights(0)
    wait_weights(1)
    c0(0)
    c1(0)
    g5(0)
    g4(1)
    c0(1)
    g6(0)
    c2(0)
    c3(0)
    g7(0)
    c4(0)
    c5(0)
    activate(0)
    wait_weights(2)
    theirs_out(0, 2)
    theirs_out(0, 1)
    g5(1)
    mine_out(0, 2)
    theirs_out(0, 3)
    mine_out(0, 1)
    mine_out(0, 3)
    r1(0)
    c1(1)
    g6(1)
    c2(1)
    theirs_out(0, 0)
    c3(1)
    mine_out(0, 0)
    g7(1)
    r2(0)
    c4(1)
    c5(1)
    activate(1)
    theirs_out(1, 2)
    theirs_out(1, 1)
    mine_out(1, 2)
    theirs_out(1, 3)
    mine_out(1, 1)
    mine_out(1, 3)
    r1(1)
    theirs_out(1, 0)
    mine_out(1, 0)
    r2_lines(1)
    r3(0)
    r3_lines(1)
    r4(0)
    r5(0)
    r5(1)
    finish(0)
    finish(1)

    for q in PAIRS:
        left_off(q, 0, planes(q, 4, False))
        left_off(q, 1, planes(q, 3, False))
        left_off(q, 2, lines(q, 3, False))
        left_off(q, 3, tiles(q, 3, False))
    at = pl.multiple_of((1 - core) * HALF, LANE)
    for s in range(STEPS):
        swap_back(s).wait()
        out[s, :, pl.ds(at, HALF)] = last_recv[s].astype(BF16)


def scatter_shapes():
    shapes = []
    for stage in (3, 2, 1):
        for s, p in PAIRS:
            _, count, order = PARTS[s][p]
            dims = tuple(4 if a in order[: stage - 1] else 1 for a in range(3))
            shapes.append(pltpu.VMEM((3,) + dims + (TILE, count * LANE), BF16))
    return shapes


def body(hidden_states, expert_routes, route_gates, gate_weights, up_weights, down_weights):
    width = hidden_states.shape[2]
    vmem = pl.BlockSpec(memory_space=pltpu.VMEM)
    hbm = pl.BlockSpec(memory_space=pl.ANY)
    pairs = len(PAIRS)
    copies = [
        pltpu.SemaphoreType.DMA((count,))
        for count in (3, 3, 3, *(pairs * k for k in (G_SENDS, G_RECVS, B_SENDS, B_RECVS)))
    ]
    return pl.pallas_call(
        kernel,
        out_shape=jax.ShapeDtypeStruct(hidden_states.shape, BF16),
        in_specs=[vmem, vmem, vmem, hbm, hbm, hbm],
        out_specs=vmem,
        scratch_shapes=[
            pltpu.VMEM((STEPS, 4, 4, 4, TILE, 2 * HALF_T), BF16),
            pltpu.VMEM((width, 2 * HIDDEN), BF16),
            pltpu.VMEM((HIDDEN, width), BF16),
            pltpu.VMEM((STEPS, 4, 4, 4, TILE, 2 * HIDDEN), F32),
            pltpu.VMEM((STEPS, 4, 4, 4, TILE, HIDDEN), BF16),
            pltpu.VMEM((8, HALF_T), F32),
            pltpu.VMEM((8, HALF_T), F32),
            pltpu.VMEM((STEPS, 4, HALF), F32),
            pltpu.VMEM((STEPS, 4, HALF), F32),
            pltpu.VMEM((STEPS, 4, 4, 4, TILE, HALF), BF16),
            *scatter_shapes(),
            *copies,
        ],
        compiler_params=pltpu.CompilerParams(
            collective_id=0, has_side_effects=True, vmem_limit_bytes=60 * 1024 * 1024
        ),
        cost_estimate=pl.CostEstimate(
            flops=11_300_000_000, bytes_accessed=12_000_000, transcendentals=262144
        ),
    )(hidden_states, expert_routes, route_gates, gate_weights, up_weights, down_weights)


def solution(mesh):
    return jax.shard_map(
        body,
        mesh=mesh,
        in_specs=(
            P(None, ("grp", "ep"), None),
            P(None, ("grp", "ep"), None),
            P(None, ("grp", "ep"), None),
            P("ep", None, "grp"),
            P("ep", None, "grp"),
            P("ep", "grp", None),
        ),
        out_specs=P(None, ("grp", "ep"), None),
        check_vma=False,
    )
```

```python
import jax
import jax.numpy as jnp
from jax import lax
from jax.experimental import pallas as pl
from jax.experimental.pallas import tpu as pltpu
from jax.sharding import PartitionSpec as P

LANE = 128
TILE = 8
UNITS = 28
HALF = UNITS * LANE
HALF_T = HALF + LANE
HIDDEN = 256
STEPS = 2
MESH = pl.DeviceIdType.MESH
F32 = jnp.float32
BF16 = jnp.bfloat16

PARTS = (
    ((0, 10, (2, 1, 0)), (10, 9, (0, 2, 1)), (19, 9, (1, 0, 2))),
    ((0, 10, (0, 2, 1)), (10, 9, (1, 0, 2)), (19, 9, (2, 1, 0))),
)
TABLE_PART = 2
N_PARTS = 3
G_SENDS, G_RECVS, B_SENDS, B_RECVS = 4, 11, 4, 15
PAIRS = tuple((s, p) for s in range(STEPS) for p in range(N_PARTS))


def part_units(q, table):
    first, count, _ = PARTS[q[0]][q[1]]
    return first, count + (1 if table and q[1] == TABLE_PART else 0)


def halves(q, table):
    first, count = part_units(q, table)
    left = (count + 1 - q[0] % 2) // 2
    return (first, left), (first + left, count - left)


def kernel(
    hs, routes, gates, wg_hbm, wu_hbm, wd_hbm,
    out,
    X, wgu, wd, h, act, zero_send, zero_recv, last_send, last_recv, R0,
    *rest,
):
    n = len(PAIRS)
    R3, R2, R1 = (dict(zip(PAIRS, rest[i * n : (i + 1) * n])) for i in range(3))
    w_sem, e_send, e_recv, g_send, g_recv, b_send, b_recv = rest[3 * n :]
    core = lax.axis_index("grp")
    ep = lax.axis_index("ep")
    me = (ep // 16, (ep // 4) % 4, ep % 4)
    sibling = (1 - core, ep)
    scale = (16, 4, 1)
    parts = range(N_PARTS)

    spots = [[lax.rem(me[axis] + d, 4) for d in range(4)] for axis in range(3)]
    peers = [
        [(core, ep + (spots[axis][d] - me[axis]) * scale[axis]) for d in range(4)] for axis in range(3)
    ]

    def place(axis, delta):
        return spots[axis][delta % 4]

    def peer(axis, delta):
        return peers[axis][delta]

    weights = [
        pltpu.make_async_copy(wg_hbm.at[0], wgu.at[:, pl.ds(0, HIDDEN)], w_sem.at[0]),
        pltpu.make_async_copy(wu_hbm.at[0], wgu.at[:, pl.ds(HIDDEN, HIDDEN)], w_sem.at[1]),
        pltpu.make_async_copy(wd_hbm.at[0], wd, w_sem.at[2]),
    ]
    for copy in weights:
        copy.start()

    barrier = pltpu.get_barrier_semaphore()
    pl.semaphore_signal(barrier, inc=1, device_id=sibling, device_id_type=MESH)
    for axis in range(3):
        for delta in (2, 1, 3):
            pl.semaphore_signal(barrier, inc=1, device_id=peer(axis, delta), device_id_type=MESH)

    lane = lax.broadcasted_iota(jnp.int32, (4, LANE), 1)

    def own_rows(c):
        at = pl.multiple_of(c * HALF, LANE)
        return jnp.concatenate(
            [hs[s, :, pl.ds(at, HALF)].astype(F32) for s in range(STEPS)], axis=0
        )

    tables = []
    for s in range(STEPS):
        total = jnp.zeros((4, LANE), F32)
        for k in range(8):
            total += jnp.where(
                lane == routes[s, :, k : k + 1], gates[s, :, k : k + 1].astype(F32), 0.0
            )
        tables.append(total)
    table = jnp.concatenate(tables, axis=0)

    zero_send[:, pl.ds(0, HALF)] = own_rows(1 - core)
    zero_send[:, pl.ds(HALF, LANE)] = table
    h[...] = jnp.zeros_like(h)
    pl.semaphore_wait(barrier, 10)
    swap = pltpu.make_async_remote_copy(
        src_ref=zero_send, dst_ref=zero_recv, send_sem=e_send.at[0], recv_sem=e_recv.at[0],
        device_id=sibling, device_id_type=MESH,
    )
    swap.start()
    base = pl.multiple_of(core * HALF_T, LANE)
    mine = jnp.concatenate([own_rows(core), table], axis=1)
    first = core == 0
    swap.wait()
    theirs = zero_recv[...]
    low, high = jnp.where(first, mine, theirs), jnp.where(first, theirs, mine)
    for s in range(STEPS):
        tile = jnp.concatenate([low[4 * s : 4 * s + 4], high[4 * s : 4 * s + 4]], axis=0)
        X[s, me[0], me[1], me[2], :, pl.ds(base, HALF_T)] = tile.astype(BF16)

    def spread(q, places):
        index = [None] * 3
        for axis, j in zip(PARTS[q[0]][q[1]][2], places):
            if j is None:
                j = pl.ds(0, 4)
            index[axis] = j if isinstance(j, pl.Slice) else pl.ds(j, 1)
        return (q[0],) + tuple(index)

    def block(q, places, c, units):
        at = pl.multiple_of(c * HALF_T + units[0] * LANE, LANE)
        return spread(q, places) + (pl.ds(0, TILE), pl.ds(at, units[1] * LANE))

    def axis_of(q, n):
        return PARTS[q[0]][q[1]][2][n]

    def near(q, n, offset):
        return place(axis_of(q, n), offset)

    def index_of(q, count, k):
        return (q[0] * N_PARTS + q[1]) * count + k

    def remote(src, dst, sends, send, recvs, recv, device):
        return pltpu.make_async_remote_copy(
            src_ref=src, dst_ref=dst, send_sem=sends.at[send], recv_sem=recvs.at[recv],
            device_id=device, device_id_type=MESH,
        )

    def wait_for(ref, sem):
        pltpu.make_async_copy(ref, ref, sem).wait()

    def sized(q, places, table):
        return X.at[block(q, places, core, part_units(q, table))]

    def tiles(q, count, table):
        return sized(q, (pl.ds(0, count), 0, 0), table)

    def lines(q, count, table):
        return sized(q, (None, pl.ds(0, count), 0), table)

    def planes(q, count, table):
        return sized(q, (None, None, pl.ds(0, count)), table)

    def some(q, stage, units):
        return X.at[block(q, ((None, None, 0) if stage == 3 else (None, 0, 0)), core, units)]

    def gather_copy(q, places, units, send, recv, device):
        ref = X.at[block(q, places, core, units)]
        return remote(ref, ref, g_send, index_of(q, G_SENDS, send), g_recv, index_of(q, G_RECVS, recv), device)

    def sent(q, send, ref):
        wait_for(ref, g_send.at[index_of(q, G_SENDS, send)])

    def came(q, recv, ref):
        wait_for(ref, g_recv.at[index_of(q, G_RECVS, recv)])

    def ring(q, stage, units, offset, to, recv):
        places = (
            (None, near(q, 1, offset), near(q, 2, 0)) if stage == 2 else (None, None, near(q, 2, offset))
        )
        gather_copy(q, places, units, stage - 1, recv, peer(axis_of(q, stage - 1), to)).start()

    def passed(q, offset, recv):
        ref = X.at[block(q, (None, None, near(q, 2, offset)), core, part_units(q, False))]
        remote(
            ref, ref, g_send, index_of(q, G_SENDS, 3), g_recv, index_of(q, G_RECVS, recv), sibling
        ).start()

    def multiply(q, offsets, c):
        units = part_units(q, False)
        rows = [
            X[block(q, (None, None, near(q, 2, o)), c, units)].reshape(16 * TILE, units[1] * LANE)
            for o in offsets
        ]
        rows = rows[0] if len(rows) == 1 else jnp.concatenate(rows, axis=0)
        at = pl.multiple_of(c * HALF + units[0] * LANE, LANE)
        found = jnp.dot(rows, wgu[pl.ds(at, units[1] * LANE), :], preferred_element_type=F32)
        for i, o in enumerate(offsets):
            where = spread(q, (None, None, near(q, 2, o)))
            h[where] += found[i * 16 * TILE : (i + 1) * 16 * TILE].reshape(h[where].shape)

    def each(step):
        def over(s):
            for p in parts:
                step((s, p))
        return over

    @each
    def g1(q):
        for d in (2, 1, 3):
            places = tuple(near(q, i, 0) for i in range(3))
            gather_copy(q, places, part_units(q, True), 0, 0, peer(axis_of(q, 0), d)).start()

    @each
    def g2(q):
        came(q, 0, tiles(q, 3, True))
        a, b = halves(q, True)
        ring(q, 2, a, 0, 1, 1)
        ring(q, 2, b, 0, 3, 2)
        ring(q, 2, b, 0, 1, 3)
        ring(q, 2, a, 0, 3, 3)

    @each
    def g3(q):
        a, b = halves(q, True)
        came(q, 1, some(q, 2, a))
        ring(q, 2, a, 3, 1, 3)
        came(q, 2, some(q, 2, b))
        ring(q, 2, b, 1, 3, 3)

    @each
    def g4(q):
        came(q, 3, lines(q, 2, True))
        a, b = halves(q, True)
        ring(q, 3, a, 0, 1, 4)
        ring(q, 3, b, 0, 3, 5)
        ring(q, 3, b, 0, 1, 6)
        ring(q, 3, a, 0, 3, 6)
        passed(q, 0, 8)

    @each
    def g5(q):
        a, b = halves(q, True)
        came(q, 4, some(q, 3, a))
        ring(q, 3, a, 3, 1, 7)
        came(q, 5, some(q, 3, b))
        ring(q, 3, b, 1, 3, 7)

    @each
    def g6(q):
        came(q, 6, planes(q, 1, True))
        passed(q, 3, 9)
        passed(q, 1, 9)

    @each
    def g7(q):
        came(q, 7, planes(q, 1, True))
        passed(q, 2, 10)

    @each
    def c0(q):
        multiply(q, (0,), core)

    @each
    def c1(q):
        came(q, 8, planes(q, 1, False))
        multiply(q, (0,), 1 - core)

    @each
    def c2(q):
        multiply(q, (3, 1), core)

    @each
    def c3(q):
        came(q, 9, planes(q, 2, False))
        multiply(q, (3, 1), 1 - core)

    @each
    def c4(q):
        multiply(q, (2,), core)

    @each
    def c5(q):
        came(q, 10, planes(q, 1, False))
        multiply(q, (2,), 1 - core)

    chosen = (lax.broadcasted_iota(jnp.int32, (LANE, HIDDEN), 0) == ep // 4).astype(BF16)
    table_at = pl.multiple_of(base + HALF, LANE)

    def activate(s):
        def one(i, carry):
            rows = X[s, i, :, :, :, pl.ds(table_at, LANE)].reshape(16 * TILE, LANE)
            scaled = jnp.dot(rows, chosen, preferred_element_type=F32)
            both = h[s, i].reshape(16 * TILE, 2 * HIDDEN)
            gate, up = both[:, :HIDDEN], both[:, HIDDEN:]
            value = gate / (1.0 + jnp.exp(-gate)) * up * scaled
            act[s, i] = value.astype(BF16).reshape(4, 4, TILE, HIDDEN)
            return carry

        lax.fori_loop(0, 4, one, 0)
        for p in parts:
            q = (s, p)
            sent(q, 0, tiles(q, 3, True))
            sent(q, 1, lines(q, 3, True))
            sent(q, 2, planes(q, 3, True))
            sent(q, 3, planes(q, 4, False))

    def down(q, offsets, c):
        first_unit, count = part_units(q, False)
        rows = [
            act[spread(q, (None, None, near(q, 2, o)))].reshape(16 * TILE, HIDDEN) for o in offsets
        ]
        rows = rows[0] if len(rows) == 1 else jnp.concatenate(rows, axis=0)
        at = pl.multiple_of(c * HALF + first_unit * LANE, LANE)
        found = jnp.dot(rows, wd[:, pl.ds(at, count * LANE)], preferred_element_type=F32)
        return [found[i * 16 * TILE : (i + 1) * 16 * TILE] for i in range(len(offsets))]

    def cross_places(q, offset, c):
        units = part_units(q, False)
        places = (None, None, near(q, 2, offset))
        to = spread(q, places) + (pl.ds(0, TILE), pl.ds(units[0] * LANE, units[1] * LANE))
        return block(q, places, c, units), to

    def scatter_copy(q, src, dst, send, recv, device):
        remote(
            src, dst, b_send, index_of(q, B_SENDS, send), b_recv, index_of(q, B_RECVS, recv), device
        ).start()

    def left_off(q, send, ref):
        wait_for(ref, b_send.at[index_of(q, B_SENDS, send)])

    def landed(q, recv, ref):
        wait_for(ref, b_recv.at[index_of(q, B_RECVS, recv)])

    def theirs_out(s, *offsets):
        for p in parts:
            q = (s, p)
            for offset, found in zip(offsets, down(q, offsets, 1 - core)):
                where, to = cross_places(q, offset, 1 - core)
                X[where] = found.astype(BF16).reshape(X[where].shape)
                scatter_copy(q, X.at[where], R0.at[to], 0, offset, sibling)

    def mine_out(s, *offsets):
        for p in parts:
            q = (s, p)
            for offset, found in zip(offsets, down(q, offsets, core)):
                where, to = cross_places(q, offset, core)
                landed(q, offset, planes(q, 1, False))
                X[where] = (found.reshape(X[where].shape) + R0[to].astype(F32)).astype(BF16)
            if 2 in offsets:
                a, b = halves(q, False)
                ring_out(q, 3, 2, a, 0, 1, 4)
                ring_out(q, 3, 2, b, 0, 3, 5)

    def span(q, units):
        return pl.ds((units[0] - part_units(q, False)[0]) * LANE, units[1] * LANE)

    every = slice(None)

    def ring_out(q, stage, offset, units, slot, to, recv):
        places = (
            (None, near(q, 1, offset), near(q, 2, 0)) if stage == 2 else (None, None, near(q, 2, offset))
        )
        buffer = (R2 if stage == 2 else R3)[q]
        dst = buffer.at[slot, every, every, every, every, span(q, units)]
        scatter_copy(
            q, X.at[block(q, places, core, units)], dst, 1 if stage == 3 else 2, recv,
            peer(axis_of(q, stage - 1), to),
        )

    def accumulate(where, terms):
        if len(terms) == 1:
            X[where] = X[where] + terms[0]
            return
        total = X[where].astype(F32)
        for term in terms:
            total += term.astype(F32)
        X[where] = total.astype(BF16)

    @each
    def r1(q):
        a, b = halves(q, False)
        ring_out(q, 3, 1, b, 1, 1, 6)
        ring_out(q, 3, 3, a, 2, 3, 6)

    def relay(q):
        a, b = halves(q, False)
        for units, offset, recv in ((a, 1, 4), (b, 3, 5)):
            landed(q, recv, some(q, 3, units))
            term = R3[q][0, :, :, :, :, span(q, units)]
            accumulate(block(q, (None, None, near(q, 2, offset)), core, units), (term,))

    @each
    def r2(q):
        a, b = halves(q, False)
        relay(q)
        ring_out(q, 3, 1, a, 1, 1, 6)
        ring_out(q, 3, 3, b, 2, 3, 6)

    @each
    def r3(q):
        landed(q, 6, planes(q, 2, False))
        where = block(q, (None, None, near(q, 2, 0)), core, part_units(q, False))
        accumulate(where, (R3[q][1], R3[q][2]))
        a, b = halves(q, False)
        ring_out(q, 2, 2, a, 0, 1, 7)
        ring_out(q, 2, 2, b, 0, 3, 8)
        ring_out(q, 2, 1, b, 1, 1, 9)
        ring_out(q, 2, 3, a, 2, 3, 9)

    def line_index(q, line):
        return spread(q, (None, near(q, 1, line), 0))[1:]

    def r2_lines(s):
        for p in parts:
            relay((s, p))
        for line in (2, 1, 3, 0):
            for p in parts:
                q = (s, p)
                for units, offset, slot in zip(halves(q, False), (1, 3), (1, 2)):
                    src = X.at[block(q, (None, near(q, 1, line), near(q, 2, offset)), core, units)]
                    dst = R3[q].at[(slot,) + line_index(q, line) + (every, span(q, units))]
                    scatter_copy(q, src, dst, 1, 11 + line, peer(axis_of(q, 2), offset))

    def r3_lines(s):
        for p in parts:
            landed((s, p), 6, planes((s, p), 1, False))
        for line in (2, 1, 3, 0):
            for p in parts:
                q = (s, p)
                landed(q, 11 + line, lines(q, 1, False))
                where = block(q, (None, near(q, 1, line), near(q, 2, 0)), core, part_units(q, False))
                accumulate(where, tuple(R3[q][(slot,) + line_index(q, line)] for slot in (1, 2)))
                if line:
                    scatter_copy(q, X.at[where], R2[q].at[line - 1], 2, 9, peer(axis_of(q, 1), line))

    @each
    def r4(q):
        a, b = halves(q, False)
        for units, offset, slot, recv in ((a, 1, 1, 7), (b, 3, 2, 8)):
            landed(q, recv, some(q, 2, units))
            term = R2[q][0, :, :, :, :, span(q, units)]
            accumulate(block(q, (None, near(q, 1, offset), near(q, 2, 0)), core, units), (term,))
            ring_out(q, 2, offset, units, slot, offset, 9)

    @each
    def r5(q):
        units = part_units(q, False)
        if q[0] == STEPS - 1:
            landed(q, 9, lines(q, 3, False))
            terms = (R2[q][0], R2[q][1], R2[q][2])
        else:
            landed(q, 9, lines(q, 2, False))
            terms = (R2[q][1], R2[q][2])
        accumulate(block(q, (None, near(q, 1, 0), near(q, 2, 0)), core, units), terms)
        for d in (2, 1, 3):
            places = (near(q, 0, d), near(q, 1, 0), near(q, 2, 0))
            src = X.at[block(q, places, core, units)]
            scatter_copy(q, src, R1[q].at[d - 1], 3, 10, peer(axis_of(q, 0), d))

    def swap_back(s):
        return pltpu.make_async_remote_copy(
            src_ref=last_send.at[s], dst_ref=last_recv.at[s], send_sem=e_send.at[1 + s],
            recv_sem=e_recv.at[1 + s], device_id=sibling, device_id_type=MESH,
        )

    def finish(s):
        pieces = []
        for p in parts:
            q = (s, p)
            units = part_units(q, False)
            where = block(q, tuple(near(q, i, 0) for i in range(3)), core, units)
            total = X[where].astype(F32).reshape(TILE, units[1] * LANE)
            landed(q, 10, tiles(q, 3, False))
            for d in (1, 2, 3):
                total += R1[q][d - 1].astype(F32).reshape(TILE, units[1] * LANE)
            pieces.append(total)
        tile = jnp.concatenate(pieces, axis=1)
        last_send[s] = jnp.where(first, tile[4:], tile[:4])
        swap_back(s).start()
        at = pl.multiple_of(core * HALF, LANE)
        out[s, :, pl.ds(at, HALF)] = jnp.where(first, tile[:4], tile[4:]).astype(BF16)

    def wait_weights(i):
        weights[i].wait()

    g1(0)
    g1(1)
    g2(0)
    g2(1)
    g3(0)
    g3(1)
    g4(0)
    wait_weights(0)
    wait_weights(1)
    c0(0)
    c1(0)
    g5(0)
    g4(1)
    c0(1)
    g6(0)
    c2(0)
    c3(0)
    g7(0)
    c4(0)
    c5(0)
    activate(0)
    wait_weights(2)
    theirs_out(0, 2)
    theirs_out(0, 1, 3)
    g5(1)
    mine_out(0, 2)
    mine_out(0, 1, 3)
    r1(0)
    c1(1)
    g6(1)
    c2(1)
    theirs_out(0, 0)
    c3(1)
    mine_out(0, 0)
    g7(1)
    r2(0)
    c4(1)
    c5(1)
    activate(1)
    theirs_out(1, 2)
    theirs_out(1, 1, 3)
    mine_out(1, 2)
    mine_out(1, 1, 3)
    r1(1)
    theirs_out(1, 0)
    mine_out(1, 0)
    r2_lines(1)
    r3(0)
    r3_lines(1)
    r4(0)
    r5(0)
    r5(1)
    finish(0)
    finish(1)

    for q in PAIRS:
        left_off(q, 0, planes(q, 4, False))
        left_off(q, 1, planes(q, 3, False))
        left_off(q, 2, lines(q, 3, False))
        left_off(q, 3, tiles(q, 3, False))
    at = pl.multiple_of((1 - core) * HALF, LANE)
    for s in range(STEPS):
        swap_back(s).wait()
        out[s, :, pl.ds(at, HALF)] = last_recv[s].astype(BF16)


def scatter_shapes():
    shapes = []
    for stage in (3, 2, 1):
        for s, p in PAIRS:
            _, count, order = PARTS[s][p]
            dims = tuple(4 if a in order[: stage - 1] else 1 for a in range(3))
            shapes.append(pltpu.VMEM((3,) + dims + (TILE, count * LANE), BF16))
    return shapes


def body(hidden_states, expert_routes, route_gates, gate_weights, up_weights, down_weights):
    width = hidden_states.shape[2]
    vmem = pl.BlockSpec(memory_space=pltpu.VMEM)
    hbm = pl.BlockSpec(memory_space=pl.ANY)
    pairs = len(PAIRS)
    copies = [
        pltpu.SemaphoreType.DMA((count,))
        for count in (3, 3, 3, *(pairs * k for k in (G_SENDS, G_RECVS, B_SENDS, B_RECVS)))
    ]
    return pl.pallas_call(
        kernel,
        out_shape=jax.ShapeDtypeStruct(hidden_states.shape, BF16),
        in_specs=[vmem, vmem, vmem, hbm, hbm, hbm],
        out_specs=vmem,
        scratch_shapes=[
            pltpu.VMEM((STEPS, 4, 4, 4, TILE, 2 * HALF_T), BF16),
            pltpu.VMEM((width, 2 * HIDDEN), BF16),
            pltpu.VMEM((HIDDEN, width), BF16),
            pltpu.VMEM((STEPS, 4, 4, 4, TILE, 2 * HIDDEN), F32),
            pltpu.VMEM((STEPS, 4, 4, 4, TILE, HIDDEN), BF16),
            pltpu.VMEM((8, HALF_T), F32),
            pltpu.VMEM((8, HALF_T), F32),
            pltpu.VMEM((STEPS, 4, HALF), F32),
            pltpu.VMEM((STEPS, 4, HALF), F32),
            pltpu.VMEM((STEPS, 4, 4, 4, TILE, HALF), BF16),
            *scatter_shapes(),
            *copies,
        ],
        compiler_params=pltpu.CompilerParams(
            collective_id=0, has_side_effects=True, vmem_limit_bytes=60 * 1024 * 1024
        ),
        cost_estimate=pl.CostEstimate(
            flops=11_300_000_000, bytes_accessed=12_000_000, transcendentals=262144
        ),
    )(hidden_states, expert_routes, route_gates, gate_weights, up_weights, down_weights)


def solution(mesh):
    return jax.shard_map(
        body,
        mesh=mesh,
        in_specs=(
            P(None, ("grp", "ep"), None),
            P(None, ("grp", "ep"), None),
            P(None, ("grp", "ep"), None),
            P("ep", None, "grp"),
            P("ep", None, "grp"),
            P("ep", "grp", None),
        ),
        out_specs=P(None, ("grp", "ep"), None),
        check_vma=False,
    )
```
